512 devices in a mesh: view: 2 (over core), gz: 32 (over z_lo, y), gy: 8 (over x, z_hi).
Axes of the slice: x: 4, y: 4, z: 16 (z_hi: 2, z_lo: 8; z = z_hi * 8 + z_lo), core: 2. Of those that a mesh axis runs over, the one named last changes fastest.
Arguments:
- observed: float32 [2, 2048, 128, 256], P('view', 'gz', 'gy'), may hold values from 0.5 to 4
- start: float32 [2048, 128, 256], P('gz', 'gy'), may hold values from 0.5 to 2
- spread_z: float32 [2, 31], P('view'), may hold values from 0.05 to 1
- spread_y: float32 [2, 7], P('view'), may hold values from 0.1 to 1
- spread_x: float32 [2, 7], P('view'), may hold values from 0.1 to 1
Outputs:
- estimate: float32 [2048, 128, 256], P('gz', 'gy')
The draws below stay inside these ranges and needn't reach their ends.
All inputs are finite; a program needn't handle non-finite values.
Results may differ from the reference program's by a relative error of at most 0.0001.
Values sent between devices are 32-bit elements; how exact they have to be, the bound alone decides.
No kernel may reach another device: no remote copies, remote signals or barrier semaphores. Data moves between devices by JAX's collectives and lax.ppermute only.
A program may use at most 64 MiB of HBM per device.

```python
import math
import jax
import jax.numpy as jnp
from jax import lax

NX = 256
KZ = 31
KY = 7
KX = 7
ITERS = 2
NZ = 2048
NY = 128
N_VIEW = 2


def level_of(own_key, extent, pieces, least, top_value):
    loudness = 1.0
    for axis_at, shards_of in pieces:
        draws = jax.random.uniform(jax.random.fold_in(jax.random.fold_in(own_key, 6), axis_at), (shards_of,), jnp.float32, least / len(pieces), top_value / len(pieces))
        loudness = loudness * jnp.repeat(jnp.exp(draws), extent[axis_at] // shards_of).reshape((-1,) + (1,) * (len(extent) - 1 - axis_at))
    return loudness


def setup_inputs(seed: int = 0) -> dict:
    key_of = jax.random.split(jax.random.key(seed), 6)
    observed = jnp.clip(jnp.exp(math.log(4.0) - 2.0794415 * jax.random.uniform(key_of[0], (N_VIEW, NZ, NY, NX), jnp.float32) ** level_of(key_of[0], (N_VIEW, NZ, NY, NX), ((0, 2), (1, 32), (2, 8)), -0.2, 0.2)), 0.5, 4.0)
    start = jnp.clip(jnp.exp(math.log(2.0) - 1.3862944 * jax.random.uniform(key_of[1], (NZ, NY, NX), jnp.float32) ** level_of(key_of[1], (NZ, NY, NX), ((0, 32), (1, 8)), -0.2, 0.2)), 0.5, 2.0)
    spread_z = jnp.clip(jnp.exp(math.log(1.0) - 2.9957323 * jax.random.uniform(key_of[2], (N_VIEW, KZ), jnp.float32) ** level_of(key_of[2], (N_VIEW, KZ), ((0, 2),), -0.2, 0.2)), 0.05, 1.0)
    spread_y = jnp.clip(jnp.exp(math.log(1.0) - 2.3025851 * jax.random.uniform(key_of[3], (N_VIEW, KY), jnp.float32) ** level_of(key_of[3], (N_VIEW, KY), ((0, 2),), -0.2, 0.2)), 0.1, 1.0)
    spread_x = jnp.clip(jnp.exp(math.log(1.0) - 2.3025851 * jax.random.uniform(key_of[4], (N_VIEW, KX), jnp.float32) ** level_of(key_of[4], (N_VIEW, KX), ((0, 2),), -0.2, 0.2)), 0.1, 1.0)
    return dict(observed=observed, start=start, spread_z=spread_z, spread_y=spread_y, spread_x=spread_x)


def correlate(field, weights, along, margin):
    padding = [(0, 0), (0, 0), (0, 0)]
    padding[along] = (margin, margin)
    padded = jnp.pad(field, padding)
    taps = weights.shape[0]
    length = padded.shape[along] - taps + 1
    total = weights[0] * lax.slice_in_dim(padded, 0, length, 1, along)
    for offset in range(1, taps):
        total = total + weights[offset] * lax.slice_in_dim(padded, offset, offset + length, 1, along)
    return total


def blur(field, weight_z, weight_y, weight_x):
    field = correlate(field, weight_z, 0, KZ // 2)
    field = correlate(field, weight_y, 1, KY // 2)
    return correlate(field, weight_x, 2, KX // 2)


def normalized(profile):
    return profile / jnp.sum(profile)


def reference(observed, start, spread_z, spread_y, spread_x):
    estimate = start
    for sweep in range(ITERS):
        summed = jnp.zeros_like(start)
        for which_view in range(2):
            weight_z = normalized(spread_z[which_view])
            weight_y = normalized(spread_y[which_view])
            weight_x = normalized(spread_x[which_view])
            blurred = blur(estimate, weight_z, weight_y, weight_x)
            quotient = observed[which_view] / blurred
            summed = summed + blur(quotient, weight_z[::-1], weight_y[::-1], weight_x[::-1])
        estimate = estimate * (0.5 * summed)
    return estimate
```

```python
import jax
import jax.numpy as jnp
from jax import lax
from jax.experimental import pallas as pl
from jax.experimental.pallas import tpu as pltpu
from jax.sharding import PartitionSpec as P

F32 = jnp.float32
BF16 = jnp.bfloat16
NX = 256
LIMIT = 56 * 1024 * 1024
VM = pl.BlockSpec(memory_space=pltpu.VMEM)
SM = pl.BlockSpec(memory_space=pltpu.SMEM)


def call(body, outs, *args, smem=1, flops=0, scratch=()):
    size = sum(a.size * a.dtype.itemsize for a in args)
    size += sum(4 * o.size for o in outs)
    return pl.pallas_call(
        body,
        out_shape=outs,
        in_specs=[SM] * smem + [VM] * (len(args) - smem),
        out_specs=[VM] * len(outs),
        scratch_shapes=list(scratch),
        compiler_params=pltpu.CompilerParams(vmem_limit_bytes=LIMIT),
        cost_estimate=pl.CostEstimate(flops=flops, bytes_accessed=size, transcendentals=0),
    )(*args)


def f32(*shape):
    return jax.ShapeDtypeStruct(shape, F32)


def b16(*shape):
    return jax.ShapeDtypeStruct(shape, BF16)


def parts(x):
    high = x.astype(BF16)
    return high, (x - high.astype(F32)).astype(BF16)


def dot(a, b):
    return jnp.dot(a, b, preferred_element_type=F32)


def rows_of(ref, half):
    return jnp.swapaxes(ref[:, 8 * half : 8 * half + 8, :], 0, 1)


def by_core(meta, body):
    for core in range(2):
        pl.when(meta[0] == core)(lambda core=core: body(core, lambda r: r % 8 if core == 0 else 7 - r % 8))


def far_body(meta, start, out_a, out_b):
    def body(core, at):
        rows = rows_of(start, core)
        for j in range(3):
            out_a[j] = rows[at(j), :32]
            out_b[j] = rows[at(j), 32:]

    by_core(meta, body)


def start_body(meta, start, e_a, e_b):
    def body(core, at):
        rows = (rows_of(start, core), rows_of(start, 1 - core))
        for j in range(11):
            e_a[j] = rows[j // 8][at(j), :32]
            e_b[j] = rows[j // 8][at(j), 32:]

    by_core(meta, body)


def observed_body(meta, observed, sz, sy, sx, mine, send):
    def body(core, at):
        rows, others = rows_of(observed, core), rows_of(observed, 1 - core)
        for j in range(8):
            mine[j] = rows[at(j)]
            send[64 * j : 64 * j + 64] = others[at(15 - j)]

    by_core(meta, body)
    send[512:520] = jnp.zeros((8, NX), F32)
    send[512:513, 0:31] = sz[...]
    send[513:514, 0:7] = sy[...]
    send[514:515, 0:7] = sx[...]


def edges_body(mine, recv, low, high):
    for j in range(8):
        low[j] = mine[j, 0:16]
        high[j] = mine[j, 48:64]
        low[8 + j] = recv[64 * j : 64 * j + 16]
        high[8 + j] = recv[64 * j + 48 : 64 * j + 64]


def weights_body(meta, own, other, zf, zb, xf, xb, yw):
    def band(shape, row, taps, place):
        d = lax.broadcasted_iota(jnp.int32, shape, 1) - lax.broadcasted_iota(jnp.int32, shape, 0)
        total = jnp.zeros(shape, F32)
        for t in range(taps):
            total = jnp.where(d == place(t), row[:, t : t + 1], total)
        return total

    for v, ref in enumerate((own, other)):
        w = ref[512:520]
        sums = jnp.sum(w, axis=1, keepdims=True)
        w = w / sums_or_one(sums)
        wz, wy, wx = w[0:1], w[1:2], w[2:3]
        high, low = parts(band((96, 128), wz, 31, lambda t: t + 1))
        zf[192 * v : 192 * v + 96, 0:128] = high
        zf[192 * v : 192 * v + 96, 128:256] = high
        zf[192 * v + 96 : 192 * v + 192, 0:128] = low
        zf[192 * v + 96 : 192 * v + 192, 128:256] = jnp.zeros((96, 128), BF16)
        high, low = parts(band((64, 96), wz, 31, lambda t: 31 - t))
        zb[v, 0:64] = jnp.concatenate([high, high], axis=1)
        zb[v, 64:128] = jnp.concatenate([low, jnp.zeros((64, 96), BF16)], axis=1)
        high, low = parts(band((256, 256), wx, 7, lambda t: 3 - t))
        xf[v, 0] = high
        xf[v, 1] = low
        high, low = parts(band((256, 256), wx, 7, lambda t: t - 3))
        xb[v, 0] = high
        xb[v, 1] = low
        for core in range(2):

            @pl.when(meta[0] == core)
            def _(core=core, v=v, wy=wy):
                for t in range(7):
                    s = t if core == 0 else 6 - t
                    yw[8 * v + t : 8 * v + t + 1, :] = jnp.broadcast_to(wy[:, s : s + 1], (1, NX))

        yw[8 * v + 7 : 8 * v + 8, :] = jnp.zeros((1, NX), F32)


def sums_or_one(sums):
    rows = lax.broadcasted_iota(jnp.int32, sums.shape, 0)
    return jnp.where(rows < 3, sums, 1.0)


def blur_z(zf, low, a, b, high):
    highs, lows = zip(*[parts(x) for x in (low, a, b, high)])
    both = dot(zf[...], jnp.concatenate(highs + lows, axis=0))
    return [both[192 * v : 192 * v + 96] + both[192 * v + 96 : 192 * v + 192] for v in range(2)]


def blur_x(x, weight, v):
    high, low = parts(x)
    return dot(high, weight[v, 0]) + dot(low, weight[v, 0]) + dot(high, weight[v, 1])


def row_result(meta, rows, recorded, yw, xf, xb, zb, v):
    total = yw[8 * v : 8 * v + 1] * rows[0]
    for t in range(1, 7):
        total = total + yw[8 * v + t : 8 * v + t + 1] * rows[t]
    blurred = blur_x(total, xf, v)
    at = lax.broadcasted_iota(jnp.int32, blurred.shape, 0)
    inside = (at >= meta[1]) & (at < meta[2])
    quotient = recorded / jnp.where(inside, blurred, 1.0)
    high, low = parts(quotient)
    both = dot(zb[v], jnp.concatenate([high, low], axis=0))
    return blur_x(both[0:64] + both[64:128], xb, v)


def recorded_row(mine, recv, o_low, o_high, j, v):
    middle = mine[j] if v == 0 else recv[64 * j : 64 * j + 64]
    return jnp.concatenate([o_low[8 * v + j], middle, o_high[8 * v + j]], axis=0)


def spread_back(yw, terms, row, planes=slice(0, 64)):
    total = None
    for v in range(2):
        for t in range(7):
            j = row + t - 3
            if 0 <= j <= 7:
                term = yw[8 * v + 6 - t : 8 * v + 7 - t] * terms(v, j)[planes]
                total = term if total is None else total + term
    return total


def early1_body(meta, e_a, e_b, e_low, e_high, mine, recv, o_low, o_high, zf, zb, xf, xb, yw, ze, bx, buf):
    for r in range(11):
        for v, x in enumerate(blur_z(zf, e_low[r], e_a[r], e_b[r], e_high[r])):
            buf[v, r] = x
            if r < 6:
                ze[v, r] = x
    for j in range(3, 8):
        for v in range(2):
            rec = recorded_row(mine, recv, o_low, o_high, j, v)
            bx[v, j - 3] = row_result(meta, [buf[v, j - 3 + t] for t in range(7)], rec, yw, xf, xb, zb, v)


def late1_body(meta, f_a, f_b, f_low, f_high, ze, bx, mine, recv, o_low, o_high, zf, zb, xf, xb, yw,
               c_far_a, c_far_b, c_mid, c_part, buf, new):
    for j in range(3):
        for v, x in enumerate(blur_z(zf, f_low[j], f_a[j], f_b[j], f_high[j])):
            buf[v, 2 - j] = x
    for j in range(3):
        for v in range(2):
            rows = [buf[v, j + t] if j + t < 3 else ze[v, j + t - 3] for t in range(7)]
            rec = recorded_row(mine, recv, o_low, o_high, j, v)
            new[v, j] = row_result(meta, rows, rec, yw, xf, xb, zb, v)

    def terms(v, j):
        return new[v, j] if j < 3 else bx[v, j - 3]

    for row in range(-3, 11):
        total = spread_back(yw, terms, row)
        if row < 3:
            c_far_a[row + 3] = total[:32]
            c_far_b[row + 3] = total[32:]
        elif row < 5:
            c_mid[row - 3] = total
        else:
            c_part[row - 5] = total


def update_mid_body(e_a, e_b, c_mid, c_part, got, out_a, out_b):
    for r in range(3, 11):
        c = c_mid[r - 3] if r < 5 else c_part[r - 5] + got[10 - r]
        out_a[r - 3] = e_a[r] * (0.5 * c[:32])
        out_b[r - 3] = e_b[r] * (0.5 * c[32:])


def update_far_body(far, e, c, got, out):
    for r in range(-3, 3):
        old = far[-1 - r] if r < 0 else e[r]
        out[r + 3] = old * (0.5 * (c[r + 3] + got[2 - r]))


def early2_body(meta, e_a, e_b, e_low, e_high, mine, recv, o_low, o_high, zf, zb, xf, xb, yw, ze, bx, buf):
    for r in range(8):
        for v, x in enumerate(blur_z(zf, e_low[r], e_a[r], e_b[r], e_high[r])):
            buf[v, r] = x
            if r < 6:
                ze[v, r] = x
    for j in (6, 7):
        for v in range(2):
            rec = recorded_row(mine, recv, o_low, o_high, j, v)
            bx[v, j - 6] = row_result(meta, [buf[v, j - 6 + t] for t in range(7)], rec, yw, xf, xb, zb, v)


def late2_body(meta, f_a, f_b, f_low, f_high, ze, mine, recv, o_low, o_high, zf, zb, xf, xb, yw,
               c_far, zn, bx):
    for r in range(6):
        for v, x in enumerate(blur_z(zf, f_low[r], f_a[r], f_b[r], f_high[r])):
            zn[v, r] = x
    for j in range(3):
        for v in range(2):
            rows = [zn[v, j + t] if j + t < 6 else ze[v, j + t - 6] for t in range(7)]
            rec = recorded_row(mine, recv, o_low, o_high, j, v)
            bx[v, j] = row_result(meta, rows, rec, yw, xf, xb, zb, v)
    for k in range(3):
        c_far[k] = spread_back(yw, lambda v, j: bx[v, j] if j < 3 else None, -1 - k)


def rest2_body(meta, zn, ze, bx0, bx6, mine, recv, o_low, o_high, zb, xf, xb, yw, c_own, c_part, new):
    for j in range(3, 6):
        for v in range(2):
            rows = [zn[v, j + t] if j + t < 6 else ze[v, j + t - 6] for t in range(7)]
            rec = recorded_row(mine, recv, o_low, o_high, j, v)
            new[v, j - 3] = row_result(meta, rows, rec, yw, xf, xb, zb, v)

    def terms(v, j):
        return bx0[v, j] if j < 3 else new[v, j - 3] if j < 6 else bx6[v, j - 6]

    for row in range(11):
        total = spread_back(yw, terms, row)
        if row < 8:
            c_own[row] = total
        else:
            c_part[row - 8] = total


def final_mid_body(e_a, e_b, c_own, got, out):
    for r in range(3, 8):
        c = c_own[r] if r < 5 else c_own[r] + got[7 - r]
        out[r - 3, :32] = e_a[r - 3] * (0.5 * c[:32])
        out[r - 3, 32:] = e_b[r - 3] * (0.5 * c[32:])


def final_far_body(f_a, f_b, c_own, got, out):
    for r in range(3):
        c = c_own[r] + got[r]
        out[r, :32] = f_a[r + 3] * (0.5 * c[:32])
        out[r, 32:] = f_b[r + 3] * (0.5 * c[32:])


def output_body(meta, far, mid, other_far, other_mid, out):
    def body(core, at):
        rows, others = [None] * 8, [None] * 8
        for r in range(8):
            rows[at(r)] = far[r] if r < 3 else mid[r - 3]
            others[at(15 - r)] = other_far[r] if r < 3 else other_mid[r - 3]
        for half, block in ((core, rows), (1 - core, others)):
            out[:, 8 * half : 8 * half + 8, :] = jnp.swapaxes(jnp.stack(block), 0, 1)

    by_core(meta, body)


def on_device(observed, start, spread_z, spread_y, spread_x):
    gy, gz = lax.axis_size("gy"), lax.axis_size("gz")
    across = [(gy + g, g + 1) for g in range(gy - 1)]
    across += [(b, a) for a, b in across]
    up = [(i, i + 1) for i in range(gz - 1)]
    down = [(j, i) for i, j in up]

    def far(x):
        return lax.ppermute(x, ("view", "gy"), across)

    def partner(x):
        return lax.ppermute(x, "view", [(0, 1), (1, 0)])

    def along_z(first, last):
        return lax.ppermute(last, "gz", up), lax.ppermute(first, "gz", down)

    at = lax.axis_index("gz")
    meta = jnp.stack(
        [lax.axis_index("view"), jnp.where(at == 0, 16, 0), jnp.where(at == gz - 1, 80, 96)]
    ).astype(jnp.int32)
    recorded = observed[0]

    send_a, send_b = call(far_body, [f32(3, 32, NX)] * 2, meta, start)
    f_a, f_b = far(send_a), far(send_b)
    mine, send = call(observed_body, [f32(8, 64, NX), f32(520, NX)], meta, recorded, spread_z, spread_y, spread_x)
    recv = partner(send)
    e_a, e_b = call(start_body, [f32(11, 32, NX)] * 2, meta, start)
    e_low, e_high = along_z(e_a, e_b)
    o_first, o_last = call(edges_body, [f32(16, 16, NX)] * 2, mine, recv, smem=0)
    o_low, o_high = along_z(o_first, o_last)
    zf, zb, xf, xb, yw = call(
        weights_body,
        [b16(384, 256), b16(2, 128, 192), b16(2, 2, 256, 256), b16(2, 2, 256, 256), f32(16, NX)],
        meta, send, recv,
    )
    obs = (mine, recv, o_low, o_high)
    f_low, f_high = along_z(f_a, f_b)

    ze, bx = call(
        early1_body, [f32(2, 6, 96, NX), f32(2, 5, 64, NX)],
        meta, e_a, e_b, e_low, e_high, *obs, zf, zb, xf, xb, yw,
        scratch=[pltpu.VMEM((2, 11, 96, NX), F32)],
    )
    c_far_a, c_far_b, c_mid, c_part = call(
        late1_body, [f32(6, 32, NX), f32(6, 32, NX), f32(2, 64, NX), f32(6, 64, NX)],
        meta, f_a, f_b, f_low, f_high, ze, bx, *obs, zf, zb, xf, xb, yw,
        scratch=[pltpu.VMEM((2, 3, 96, NX), F32), pltpu.VMEM((2, 3, 64, NX), F32)],
    )
    got_a, got_b = far(c_far_a), far(c_far_b)
    got = partner(c_part)
    m_a, m_b = call(update_mid_body, [f32(8, 32, NX)] * 2, e_a, e_b, c_mid, c_part, got, smem=0)
    m_low, m_high = along_z(m_a, m_b)
    ze, bx6 = call(
        early2_body, [f32(2, 6, 96, NX), f32(2, 2, 64, NX)],
        meta, m_a, m_b, m_low, m_high, *obs, zf, zb, xf, xb, yw,
        scratch=[pltpu.VMEM((2, 8, 96, NX), F32)],
    )
    (n_a,) = call(update_far_body, [f32(6, 32, NX)], f_a, e_a, c_far_a, got_a, smem=0)
    n_high = lax.ppermute(n_a, "gz", down)
    (n_b,) = call(update_far_body, [f32(6, 32, NX)], f_b, e_b, c_far_b, got_b, smem=0)
    n_low = lax.ppermute(n_b, "gz", up)
    c_far, zn, bx0 = call(
        late2_body, [f32(3, 64, NX), f32(2, 6, 96, NX), f32(2, 3, 64, NX)],
        meta, n_a, n_b, n_low, n_high, ze, *obs, zf, zb, xf, xb, yw,
    )
    got_far = far(c_far)
    c_own, c_part = call(
        rest2_body, [f32(8, 64, NX), f32(3, 64, NX)],
        meta, zn, ze, bx0, bx6, *obs, zb, xf, xb, yw,
        scratch=[pltpu.VMEM((2, 3, 64, NX), F32)],
    )
    got_part = partner(c_part)
    (mid,) = call(final_mid_body, [f32(5, 64, NX)], m_a, m_b, c_own, got_part, smem=0)
    other_mid = partner(mid)
    (last,) = call(final_far_body, [f32(3, 64, NX)], n_a, n_b, c_own, got_far, smem=0)
    other_last = partner(last)
    (out,) = call(output_body, [f32(64, 16, NX)], meta, last, mid, other_last, other_mid)
    return out


def solution(mesh):
    return jax.shard_map(
        on_device,
        mesh=mesh,
        in_specs=(
            P("view", "gz", "gy", None),
            P("gz", "gy", None),
            P("view", None),
            P("view", None),
            P("view", None),
        ),
        out_specs=P("gz", "gy", None),
        check_vma=False,
    )
```

```python
import jax
import jax.numpy as jnp
from jax import lax
from jax.experimental import pallas as pl
from jax.experimental.pallas import tpu as pltpu
from jax.sharding import PartitionSpec as P

F32 = jnp.float32
BF16 = jnp.bfloat16
NX = 256
LIMIT = 20 * 1024 * 1024
VM = pl.BlockSpec(memory_space=pltpu.VMEM)
SM = pl.BlockSpec(memory_space=pltpu.SMEM)


def call(body, outs, *args, smem=1, flops=0, scratch=()):
    size = sum(a.size * a.dtype.itemsize for a in args)
    size += sum(4 * o.size for o in outs)
    return pl.pallas_call(
        body,
        out_shape=outs,
        in_specs=[SM] * smem + [VM] * (len(args) - smem),
        out_specs=[VM] * len(outs),
        scratch_shapes=list(scratch),
        compiler_params=pltpu.CompilerParams(vmem_limit_bytes=LIMIT),
        cost_estimate=pl.CostEstimate(flops=0, bytes_accessed=0, transcendentals=0),
    )(*args)


def f32(*shape):
    return jax.ShapeDtypeStruct(shape, F32)


def b16(*shape):
    return jax.ShapeDtypeStruct(shape, BF16)


def parts(x):
    high = x.astype(BF16)
    return high, (x - high.astype(F32)).astype(BF16)


def dot(a, b):
    return jnp.dot(a, b, preferred_element_type=F32)


def rows_of(ref, half):
    return jnp.swapaxes(ref[:, 8 * half : 8 * half + 8, :], 0, 1)


def by_core(meta, body):
    for core in range(2):
        pl.when(meta[0] == core)(lambda core=core: body(core, lambda r: r % 8 if core == 0 else 7 - r % 8))


def far_body(meta, start, out):
    def body(core, at):
        rows = rows_of(start, core)
        for j in range(3):
            out[j] = rows[at(j)]

    by_core(meta, body)


def start_body(meta, start, e_a, e_b):
    def body(core, at):
        rows = (rows_of(start, core), rows_of(start, 1 - core))
        for j in range(11):
            e_a[j] = rows[j // 8][at(j), :32]
            e_b[j] = rows[j // 8][at(j), 32:]

    by_core(meta, body)


def observed_body(meta, e_a, e_b, observed, mine, send_a, send_b, low, high):
    def body(core, at):
        rows, others = rows_of(observed, core), rows_of(observed, 1 - core)
        for j in range(8):
            row, other = rows[at(j)], others[at(15 - j)]
            mine[j] = row
            if j < 4:
                send_a[j] = other
            else:
                send_b[j - 4] = other
            for k, x in ((j, row), (8 + j, other)):
                low[352 + 16 * k : 368 + 16 * k] = x[0:16]
                high[352 + 16 * k : 368 + 16 * k] = x[48:64]

    by_core(meta, body)
    for j in range(11):
        low[32 * j : 32 * j + 32] = e_a[j]
        high[32 * j : 32 * j + 32] = e_b[j]


def collect_body(meta, mine, got_a, got_b, obs):
    other = 1 - meta[0]
    obs[meta[0]] = mine[...]
    obs[other, 0:4] = got_a[other]
    obs[other, 4:8] = got_b[other]


def margins_body(g_low, g_high, send):
    for j in range(8):
        send[j, 0:16] = g_low[480 + 16 * j : 496 + 16 * j]
        send[j, 16:32] = g_high[480 + 16 * j : 496 + 16 * j]


def halves_body(far, _, a, b):
    for j in range(3):
        a[j] = far[j, :32]
        b[j] = far[j, 32:]


def profiles_body(sz, sy, sx, out):
    out[...] = jnp.zeros((8, NX), F32)
    out[0:1, 0:31] = sz[...]
    out[1:2, 0:7] = sy[...]
    out[2:3, 0:7] = sx[...]


def weights_body(meta, both, zf, zb, xf, xb, yw):
    def band(shape, row, taps, place, shift=lambda j: j):
        d = shift(lax.broadcasted_iota(jnp.int32, shape, 1)) - lax.broadcasted_iota(jnp.int32, shape, 0)
        total = jnp.zeros(shape, F32)
        for t in range(taps):
            total = jnp.where(d == place(t), row[:, t : t + 1], total)
        return total

    for v in range(2):
        w = both[v]
        sums = jnp.sum(w, axis=1, keepdims=True)
        w = w / sums_or_one(sums)
        wz, wy, wx = w[0:1], w[1:2], w[2:3]
        high, low = parts(band((96, 128), wz, 31, lambda t: t + 1))
        zf[192 * v : 192 * v + 96, 0:128] = high
        zf[192 * v : 192 * v + 96, 128:256] = high
        zf[192 * v + 96 : 192 * v + 192, 0:128] = low
        zf[192 * v + 96 : 192 * v + 192, 128:256] = jnp.zeros((96, 128), BF16)
        for first, width, shift in ((0, 64, lambda j: j), (128, 32, lambda j: jnp.where(j < 16, j - 16, j + 48))):
            high, low = parts(band((64, width), wz, 31, lambda t: 15 - t, shift))
            zb[v, 0:64, first : first + width] = high
            zb[v, 0:64, first + width : first + 2 * width] = high
            zb[v, 64:128, first : first + width] = low
            zb[v, 64:128, first + width : first + 2 * width] = jnp.zeros((64, width), BF16)
        high, low = parts(band((256, 256), wx, 7, lambda t: 3 - t))
        xf[v, 0] = high
        xf[v, 1] = low
        high, low = parts(band((256, 256), wx, 7, lambda t: t - 3))
        xb[v, 0] = high
        xb[v, 1] = low
        for core in range(2):

            @pl.when(meta[0] == core)
            def _(core=core, v=v, wy=wy):
                for t in range(7):
                    s = t if core == 0 else 6 - t
                    yw[8 * v + t : 8 * v + t + 1, :] = jnp.broadcast_to(wy[:, s : s + 1], (1, NX))

        yw[8 * v + 7 : 8 * v + 8, :] = jnp.zeros((1, NX), F32)


def sums_or_one(sums):
    rows = lax.broadcasted_iota(jnp.int32, sums.shape, 0)
    return jnp.where(rows < 3, sums, 1.0)


def blur_z(zf, low, a, b, high):
    highs, lows = zip(*[parts(x) for x in (low, a, b, high)])
    both = dot(zf[...], jnp.concatenate(highs + lows, axis=0))
    return [both[192 * v : 192 * v + 96] + both[192 * v + 96 : 192 * v + 192] for v in range(2)]


def blur_x(x, weight, v):
    high, low = parts(x)
    return dot(high, weight[v, 0]) + dot(low, weight[v, 0]) + dot(high, weight[v, 1])


def quotient(rows, recorded, yw, xf, v, inside=None):
    total = yw[8 * v : 8 * v + 1] * rows[0]
    for t in range(1, 7):
        total = total + yw[8 * v + t : 8 * v + t + 1] * rows[t]
    blurred = blur_x(total, xf, v)
    return recorded / (blurred if inside is None else jnp.where(inside(blurred.shape), blurred, 1.0))


def margin_inside(meta):
    def inside(shape):
        at = lax.broadcasted_iota(jnp.int32, shape, 0)
        return (at >= meta[1]) & (at < meta[2])

    return inside


def margins(rows):
    return jnp.concatenate([rows[0:16], rows[80:96]], axis=0)


def back_own(q, zb, xb, v):
    both = dot(zb[v, :, 0:128], jnp.concatenate(parts(q), axis=0))
    return blur_x(both[0:64] + both[64:128], xb, v)


def back_margins(q, zb, xb, v):
    both = dot(zb[v, :, 128:192], jnp.concatenate(parts(q), axis=0))
    both = both[0:64] + both[64:128]
    return blur_x(jnp.concatenate([both[0:16], both[48:64]], axis=0), xb, v)


def row_result(meta, rows, obs, margin, yw, xf, xb, zb, j, v):
    own = quotient([r[16:80] for r in rows], obs[v, j], yw, xf, v)
    out = quotient([margins(r) for r in rows], margin[v, j], yw, xf, v, margin_inside(meta))
    both = dot(zb[v], jnp.concatenate(parts(own) + parts(out), axis=0))
    return blur_x(both[0:64] + both[64:128], xb, v)


def spread_back(yw, terms, row, planes=slice(0, 64)):
    total = None
    for v in range(2):
        for t in range(7):
            j = row + t - 3
            if 0 <= j <= 7:
                term = yw[8 * v + 6 - t : 8 * v + 7 - t] * terms(v, j)[planes]
                total = term if total is None else total + term
    return total


def early1_body(e_a, e_b, obs, g_low, g_high, zf, zb, xf, xb, yw, ze, bx):
    for r in range(11):
        low, high = g_low[32 * r : 32 * r + 32], g_high[32 * r : 32 * r + 32]
        for v, x in enumerate(blur_z(zf, low, e_a[r], e_b[r], high)):
            ze[v, r] = x
    for j in range(3, 6):
        for v in range(2):
            q = quotient([ze[v, j - 3 + t, 16:80] for t in range(7)], obs[v, j], yw, xf, v)
            bx[v, j - 3] = back_own(q, zb, xb, v)


def late1_body(f, f_low, f_high, ze, bx, obs, zf, zb, xf, xb, yw, c_far, zn, new):
    for j in range(3):
        for v, x in enumerate(blur_z(zf, f_low[j], f[j, :32], f[j, 32:], f_high[j])):
            zn[v, 2 - j] = x
    for j in range(3):
        for v in range(2):
            rows = [zn[v, j + t, 16:80] if j + t < 3 else ze[v, j + t - 3, 16:80] for t in range(7)]
            new[v, j] = back_own(quotient(rows, obs[v, j], yw, xf, v), zb, xb, v)
    for row in range(-3, 3):
        c_far[row + 3] = spread_back(yw, lambda v, j: new[v, j] if j < 3 else bx[v, j - 3], row, slice(16, 48))


def rest1_body(meta, ze, zn, bx0, bx3, obs, g_low, g_high, got, zb, xf, xb, yw, c_far, c_mid, c_part, margin, new):
    other = 1 - meta[0]
    margin[other] = got[other]
    for j in range(8):
        margin[meta[0], j, 0:16] = g_low[352 + 16 * j : 368 + 16 * j]
        margin[meta[0], j, 16:32] = g_high[352 + 16 * j : 368 + 16 * j]
    for j in range(8):
        for v in range(2):
            rows = [zn[v, j + t] if j + t < 3 else ze[v, j + t - 3] for t in range(7)]
            if j < 6:
                own = bx0[v, j] if j < 3 else bx3[v, j - 3]
                q = quotient([margins(r) for r in rows], margin[v, j], yw, xf, v, margin_inside(meta))
                edge = back_margins(q, zb, xb, v)
                new[v, j, 0:16] = own[0:16] + edge[0:16]
                new[v, j, 16:48] = own[16:48]
                new[v, j, 48:64] = own[48:64] + edge[16:32]
            else:
                new[v, j] = row_result(meta, rows, obs, margin, yw, xf, xb, zb, j, v)
    for row in range(-3, 11):
        total = spread_back(yw, lambda v, j: new[v, j], row)
        if row < 3:
            c_far[row + 3, 0:16] = total[0:16]
            c_far[row + 3, 16:32] = total[48:64]
        elif row < 5:
            c_mid[row - 3] = total
        else:
            c_part[row - 5] = total


def update_mid_body(meta, e_a, e_b, c_mid, c_part, got, _, out_a, out_b):
    for r in range(3, 11):
        c = c_mid[r - 3] if r < 5 else c_part[r - 5] + got[1 - meta[0], 10 - r]
        out_a[r - 3] = e_a[r] * (0.5 * c[:32])
        out_b[r - 3] = e_b[r] * (0.5 * c[32:])


def update_far_body(far, e_a, e_b, c_mid, c_edge, got_mid, got_edge, out_a, out_b):
    for r in range(-3, 3):
        mid = 0.5 * (c_mid[r + 3] + got_mid[2 - r])
        edge = 0.5 * (c_edge[r + 3] + got_edge[2 - r])
        old_a = far[-1 - r, 0:32] if r < 0 else e_a[r]
        old_b = far[-1 - r, 32:64] if r < 0 else e_b[r]
        out_a[r + 3] = old_a * jnp.concatenate([edge[0:16], mid[0:16]], axis=0)
        out_b[r + 3] = old_b * jnp.concatenate([mid[16:32], edge[16:32]], axis=0)


def early2_body(meta, e_a, e_b, e_low, e_high, obs, margin, zf, zb, xf, xb, yw, ze, bx, buf):
    for r in range(8):
        for v, x in enumerate(blur_z(zf, e_low[r], e_a[r], e_b[r], e_high[r])):
            buf[v, r] = x
            if r < 6:
                ze[v, r] = x
    for j in (6, 7):
        for v in range(2):
            rows = [buf[v, j - 6 + t] for t in range(7)]
            bx[v, j - 6] = row_result(meta, rows, obs, margin, yw, xf, xb, zb, j, v)


def late2_body(meta, f_a, f_b, f_low, f_high, ze, obs, margin, zf, zb, xf, xb, yw, c_far, zn, bx):
    for r in range(6):
        for v, x in enumerate(blur_z(zf, f_low[r], f_a[r], f_b[r], f_high[r])):
            zn[v, r] = x
    for j in range(3):
        for v in range(2):
            rows = [zn[v, j + t] if j + t < 6 else ze[v, j + t - 6] for t in range(7)]
            bx[v, j] = row_result(meta, rows, obs, margin, yw, xf, xb, zb, j, v)
    for k in range(3):
        c_far[k] = spread_back(yw, lambda v, j: bx[v, j] if j < 3 else None, -1 - k)


def rest2_body(meta, zn, ze, bx0, bx6, obs, margin, zb, xf, xb, yw, c_own, c_part, new):
    for j in range(3, 6):
        for v in range(2):
            rows = [zn[v, j + t] if j + t < 6 else ze[v, j + t - 6] for t in range(7)]
            new[v, j - 3] = row_result(meta, rows, obs, margin, yw, xf, xb, zb, j, v)

    def terms(v, j):
        return bx0[v, j] if j < 3 else new[v, j - 3] if j < 6 else bx6[v, j - 6]

    for row in range(11):
        total = spread_back(yw, terms, row)
        if row < 8:
            c_own[row] = total
        else:
            c_part[row - 8] = total


def final_mid_body(meta, e_a, e_b, c_own, got, out):
    for r in range(3, 8):
        c = c_own[r] if r < 5 else c_own[r] + got[1 - meta[0], 7 - r]
        out[r - 3, :32] = e_a[r - 3] * (0.5 * c[:32])
        out[r - 3, 32:] = e_b[r - 3] * (0.5 * c[32:])


def final_far_body(f_a, f_b, c_own, got, out):
    for r in range(3):
        c = c_own[r] + got[r]
        out[r, :32] = f_a[r + 3] * (0.5 * c[:32])
        out[r, 32:] = f_b[r + 3] * (0.5 * c[32:])


def output_body(meta, far, mid, out):
    def body(core, at):
        for c in range(2):
            block = [far[c, r] if r < 3 else mid[c, r - 3] for r in range(8)]
            block = block if c == 0 else block[::-1]
            out[:, 8 * c : 8 * c + 8, :] = jnp.swapaxes(jnp.stack(block), 0, 1)

    body(0, None)


def on_device(observed, start, spread_z, spread_y, spread_x):
    gy, gz = lax.axis_size("gy"), lax.axis_size("gz")
    across = [(gy + g, g + 1) for g in range(gy - 1)]
    across += [(b, a) for a, b in across]
    up = [(i, i + 1) for i in range(gz - 1)]
    down = [(j, i) for i, j in up]

    def far(x):
        return lax.ppermute(x, ("view", "gy"), across)

    def both(x):
        return lax.all_gather(x, "view")

    def along_z(first, last):
        return lax.ppermute(last, "gz", up), lax.ppermute(first, "gz", down)

    def place():
        at = lax.axis_index("gz")
        limits = [jnp.where(at == 0, 16, 0), jnp.where(at == gz - 1, 16, 32)]
        return jnp.stack([lax.axis_index("view"), *limits]).astype(jnp.int32)

    meta = place()
    recorded = observed[0]

    (send_far,) = call(far_body, [f32(3, 64, NX)], meta, start)
    f = far(send_far)

    def beside(start, recorded, spread_z, spread_y, spread_x):
        meta = place()
        e_a, e_b = call(start_body, [f32(11, 32, NX)] * 2, meta, start)
        mine, send_a, send_b, first, last = call(
            observed_body,
            [f32(8, 64, NX), f32(4, 64, NX), f32(4, 64, NX), f32(608, NX), f32(608, NX)],
            meta, e_a, e_b, recorded,
        )
        g_low, g_high = along_z(first, last)
        (obs,) = call(collect_body, [f32(2, 8, 64, NX)], meta, mine, both(send_a), both(send_b))
        (profiles,) = call(profiles_body, [f32(8, NX)], spread_z, spread_y, spread_x, smem=0)
        weights = call(
            weights_body,
            [b16(384, 256), b16(2, 128, 192), b16(2, 2, 256, 256), b16(2, 2, 256, 256), f32(16, NX)],
            meta, both(profiles),
        )
        return e_a, e_b, obs, g_low, g_high, *weights

    args = (start, recorded, spread_z, spread_y, spread_x)
    shapes = jax.eval_shape(beside, *args)
    e_a, e_b, obs, g_low, g_high, zf, zb, xf, xb, yw = lax.cond(
        lax.axis_index("gz") < gz, beside, lambda *a: tuple(jnp.zeros(x.shape, x.dtype) for x in shapes), *args
    )
    f_low, f_high = along_z(*call(halves_body, [f32(3, 32, NX)] * 2, f, yw, smem=0))
    ze, bx3 = call(
        early1_body, [f32(2, 11, 96, NX), f32(2, 3, 64, NX)],
        e_a, e_b, obs, g_low, g_high, zf, zb, xf, xb, yw, smem=0,
    )
    c_far_mid, zn, bx0 = call(
        late1_body, [f32(6, 32, NX), f32(2, 3, 96, NX), f32(2, 3, 64, NX)],
        f, f_low, f_high, ze, bx3, obs, zf, zb, xf, xb, yw, smem=0,
    )
    got_mid = far(c_far_mid)
    (send,) = call(margins_body, [f32(8, 32, NX)], g_low, g_high, smem=0)
    c_far_edge, c_mid, c_part, margin = call(
        rest1_body, [f32(6, 32, NX), f32(2, 64, NX), f32(6, 64, NX), f32(2, 8, 32, NX)],
        meta, ze, zn, bx0, bx3, obs, g_low, g_high, both(send), zb, xf, xb, yw,
        scratch=[pltpu.VMEM((2, 8, 64, NX), F32)],
    )
    got_edge = far(c_far_edge)
    obs = (obs, margin)
    got = both(c_part)
    m_a, m_b = call(update_mid_body, [f32(8, 32, NX)] * 2, meta, e_a, e_b, c_mid, c_part, got, got_mid)
    m_low, m_high = along_z(m_a, m_b)
    ze, bx6 = call(
        early2_body, [f32(2, 6, 96, NX), f32(2, 2, 64, NX)],
        meta, m_a, m_b, m_low, m_high, *obs, zf, zb, xf, xb, yw,
        scratch=[pltpu.VMEM((2, 8, 96, NX), F32)],
    )
    n_a, n_b = call(
        update_far_body, [f32(6, 32, NX)] * 2, f, e_a, e_b, c_far_mid, c_far_edge, got_mid, got_edge, smem=0
    )
    n_low, n_high = along_z(n_a, n_b)
    c_far, zn, bx0 = call(
        late2_body, [f32(3, 64, NX), f32(2, 6, 96, NX), f32(2, 3, 64, NX)],
        meta, n_a, n_b, n_low, n_high, ze, *obs, zf, zb, xf, xb, yw,
    )
    got_far = far(c_far)
    c_own, c_part = call(
        rest2_body, [f32(8, 64, NX), f32(3, 64, NX)],
        meta, zn, ze, bx0, bx6, *obs, zb, xf, xb, yw,
        scratch=[pltpu.VMEM((2, 3, 64, NX), F32)],
    )
    got_part = both(c_part)
    (mid,) = call(final_mid_body, [f32(5, 64, NX)], meta, m_a, m_b, c_own, got_part)
    other_mid = both(mid)
    (last,) = call(final_far_body, [f32(3, 64, NX)], n_a, n_b, c_own, got_far, smem=0)
    other_last = both(last)
    (out,) = call(output_body, [f32(64, 16, NX)], meta, other_last, other_mid)
    return out


def solution(mesh):
    return jax.shard_map(
        on_device,
        mesh=mesh,
        in_specs=(
            P("view", "gz", "gy", None),
            P("gz", "gy", None),
            P("view", None),
            P("view", None),
            P("view", None),
        ),
        out_specs=P("gz", "gy", None),
        check_vma=False,
    )
```

```python
import jax
import jax.numpy as jnp
from jax import lax
from jax.experimental import pallas as pl
from jax.experimental.pallas import tpu as pltpu
from jax.sharding import PartitionSpec as P

F32 = jnp.float32
BF16 = jnp.bfloat16
NX = 256
LIMIT = 20 * 1024 * 1024
VM = pl.BlockSpec(memory_space=pltpu.VMEM)
SM = pl.BlockSpec(memory_space=pltpu.SMEM)


def call(body, outs, *args, smem=1, flops=0, scratch=()):
    size = sum(a.size * a.dtype.itemsize for a in args)
    size += sum(4 * o.size for o in outs)
    return pl.pallas_call(
        body,
        out_shape=outs,
        in_specs=[SM] * smem + [VM] * (len(args) - smem),
        out_specs=[VM] * len(outs),
        scratch_shapes=list(scratch),
        compiler_params=pltpu.CompilerParams(vmem_limit_bytes=LIMIT),
        cost_estimate=pl.CostEstimate(flops=0, bytes_accessed=0, transcendentals=0),
    )(*args)


def f32(*shape):
    return jax.ShapeDtypeStruct(shape, F32)


def b16(*shape):
    return jax.ShapeDtypeStruct(shape, BF16)


def parts(x):
    high = x.astype(BF16)
    return high, (x - high.astype(F32)).astype(BF16)


def dot(a, b):
    return jnp.dot(a, b, preferred_element_type=F32)


def rows_of(ref, half):
    return jnp.swapaxes(ref[:, 8 * half : 8 * half + 8, :], 0, 1)


def by_core(meta, body):
    for core in range(2):
        pl.when(meta[0] == core)(lambda core=core: body(core, lambda r: r % 8 if core == 0 else 7 - r % 8))


def far_body(meta, start, out):
    def body(core, at):
        rows = rows_of(start, core)
        for j in range(3):
            out[j] = rows[at(j)]

    by_core(meta, body)


def start_body(meta, start, e_a, e_b):
    def body(core, at):
        rows = (rows_of(start, core), rows_of(start, 1 - core))
        for j in range(11):
            e_a[j] = rows[j // 8][at(j), :32]
            e_b[j] = rows[j // 8][at(j), 32:]

    by_core(meta, body)


def observed_body(meta, observed, mine, send_a, send_b):
    def body(core, at):
        rows, others = rows_of(observed, core), rows_of(observed, 1 - core)
        for j in range(8):
            mine[j] = rows[at(j)]
            if j < 4:
                send_a[j] = others[at(15 - j)]
            else:
                send_b[j - 4] = others[at(15 - j)]

    by_core(meta, body)


def profiles_body(sz, sy, sx, out):
    out[...] = jnp.zeros((8, NX), F32)
    out[0:1, 0:31] = sz[...]
    out[1:2, 0:7] = sy[...]
    out[2:3, 0:7] = sx[...]


def edges_body(meta, mine, got_a, got_b, obs, low, high):
    other = 1 - meta[0]
    for j in range(8):
        for v, row in ((meta[0], mine[j]), (other, got_a[other, j] if j < 4 else got_b[other, j - 4])):
            obs[v, j] = row
            low[v, j] = row[0:16]
            high[v, j] = row[48:64]


def faces_body(far, _, first, last):
    for j in range(3):
        first[j] = far[j, 0:32]
        last[j] = far[j, 32:64]


def weights_body(meta, both, zf, zb, xf, xb, yw):
    def band(shape, row, taps, place):
        d = lax.broadcasted_iota(jnp.int32, shape, 1) - lax.broadcasted_iota(jnp.int32, shape, 0)
        total = jnp.zeros(shape, F32)
        for t in range(taps):
            total = jnp.where(d == place(t), row[:, t : t + 1], total)
        return total

    for v in range(2):
        w = both[v]
        sums = jnp.sum(w, axis=1, keepdims=True)
        w = w / sums_or_one(sums)
        wz, wy, wx = w[0:1], w[1:2], w[2:3]
        high, low = parts(band((96, 128), wz, 31, lambda t: t + 1))
        zf[192 * v : 192 * v + 96, 0:128] = high
        zf[192 * v : 192 * v + 96, 128:256] = high
        zf[192 * v + 96 : 192 * v + 192, 0:128] = low
        zf[192 * v + 96 : 192 * v + 192, 128:256] = jnp.zeros((96, 128), BF16)
        high, low = parts(band((64, 96), wz, 31, lambda t: 31 - t))
        zb[v, 0:64] = jnp.concatenate([high, high], axis=1)
        zb[v, 64:128] = jnp.concatenate([low, jnp.zeros((64, 96), BF16)], axis=1)
        high, low = parts(band((256, 256), wx, 7, lambda t: 3 - t))
        xf[v, 0] = high
        xf[v, 1] = low
        high, low = parts(band((256, 256), wx, 7, lambda t: t - 3))
        xb[v, 0] = high
        xb[v, 1] = low
        for core in range(2):

            @pl.when(meta[0] == core)
            def _(core=core, v=v, wy=wy):
                for t in range(7):
                    s = t if core == 0 else 6 - t
                    yw[8 * v + t : 8 * v + t + 1, :] = jnp.broadcast_to(wy[:, s : s + 1], (1, NX))

        yw[8 * v + 7 : 8 * v + 8, :] = jnp.zeros((1, NX), F32)


def sums_or_one(sums):
    rows = lax.broadcasted_iota(jnp.int32, sums.shape, 0)
    return jnp.where(rows < 3, sums, 1.0)


def blur_z(zf, low, a, b, high):
    highs, lows = zip(*[parts(x) for x in (low, a, b, high)])
    both = dot(zf[...], jnp.concatenate(highs + lows, axis=0))
    return [both[192 * v : 192 * v + 96] + both[192 * v + 96 : 192 * v + 192] for v in range(2)]


def blur_x(x, weight, v):
    high, low = parts(x)
    return dot(high, weight[v, 0]) + dot(low, weight[v, 0]) + dot(high, weight[v, 1])


def row_result(meta, rows, recorded, yw, xf, xb, zb, v):
    total = yw[8 * v : 8 * v + 1] * rows[0]
    for t in range(1, 7):
        total = total + yw[8 * v + t : 8 * v + t + 1] * rows[t]
    blurred = blur_x(total, xf, v)
    at = lax.broadcasted_iota(jnp.int32, blurred.shape, 0)
    inside = (at >= meta[1]) & (at < meta[2])
    quotient = recorded / jnp.where(inside, blurred, 1.0)
    high, low = parts(quotient)
    both = dot(zb[v], jnp.concatenate([high, low], axis=0))
    return blur_x(both[0:64] + both[64:128], xb, v)


def recorded_row(obs, o_low, o_high, j, v):
    return jnp.concatenate([o_low[v, j], obs[v, j], o_high[v, j]], axis=0)


def spread_back(yw, terms, row, planes=slice(0, 64)):
    total = None
    for v in range(2):
        for t in range(7):
            j = row + t - 3
            if 0 <= j <= 7:
                term = yw[8 * v + 6 - t : 8 * v + 7 - t] * terms(v, j)[planes]
                total = term if total is None else total + term
    return total


def early1_body(e_a, e_b, e_low, e_high, zf, ze):
    for r in range(11):
        for v, x in enumerate(blur_z(zf, e_low[r], e_a[r], e_b[r], e_high[r])):
            ze[v, r] = x


def middle1_body(meta, ze, obs, o_low, o_high, zb, xf, xb, yw, bx):
    for j in range(3, 8):
        for v in range(2):
            rec = recorded_row(obs, o_low, o_high, j, v)
            bx[v, j - 3] = row_result(meta, [ze[v, j - 3 + t] for t in range(7)], rec, yw, xf, xb, zb, v)


def late1_body(meta, f, f_low, f_high, ze, bx, obs, o_low, o_high, zf, zb, xf, xb, yw,
               c_far, c_mid, c_part, buf, new):
    for j in range(3):
        for v, x in enumerate(blur_z(zf, f_low[j], f[j, :32], f[j, 32:], f_high[j])):
            buf[v, 2 - j] = x
    for j in range(3):
        for v in range(2):
            rows = [buf[v, j + t] if j + t < 3 else ze[v, j + t - 3] for t in range(7)]
            rec = recorded_row(obs, o_low, o_high, j, v)
            new[v, j] = row_result(meta, rows, rec, yw, xf, xb, zb, v)

    def terms(v, j):
        return new[v, j] if j < 3 else bx[v, j - 3]

    for row in range(-3, 11):
        total = spread_back(yw, terms, row)
        if row < 3:
            c_far[row + 3] = total
        elif row < 5:
            c_mid[row - 3] = total
        else:
            c_part[row - 5] = total


def update_mid_body(meta, e_a, e_b, c_mid, c_part, got, out_a, out_b):
    for r in range(3, 11):
        c = c_mid[r - 3] if r < 5 else c_part[r - 5] + got[1 - meta[0], 10 - r]
        out_a[r - 3] = e_a[r] * (0.5 * c[:32])
        out_b[r - 3] = e_b[r] * (0.5 * c[32:])


def update_far_body(far, e_a, e_b, c, got, out_a, out_b):
    for r in range(-3, 3):
        factor = 0.5 * (c[r + 3] + got[2 - r])
        out_a[r + 3] = (far[-1 - r, :32] if r < 0 else e_a[r]) * factor[:32]
        out_b[r + 3] = (far[-1 - r, 32:] if r < 0 else e_b[r]) * factor[32:]


def early2_body(meta, e_a, e_b, e_low, e_high, obs, o_low, o_high, zf, zb, xf, xb, yw, ze, bx, buf):
    for r in range(8):
        for v, x in enumerate(blur_z(zf, e_low[r], e_a[r], e_b[r], e_high[r])):
            buf[v, r] = x
            if r < 6:
                ze[v, r] = x
    for j in (6, 7):
        for v in range(2):
            rec = recorded_row(obs, o_low, o_high, j, v)
            bx[v, j - 6] = row_result(meta, [buf[v, j - 6 + t] for t in range(7)], rec, yw, xf, xb, zb, v)


def late2_body(meta, f_a, f_b, f_low, f_high, ze, obs, o_low, o_high, zf, zb, xf, xb, yw,
               c_far, zn, bx):
    for r in range(6):
        for v, x in enumerate(blur_z(zf, f_low[r], f_a[r], f_b[r], f_high[r])):
            zn[v, r] = x
    for j in range(3):
        for v in range(2):
            rows = [zn[v, j + t] if j + t < 6 else ze[v, j + t - 6] for t in range(7)]
            rec = recorded_row(obs, o_low, o_high, j, v)
            bx[v, j] = row_result(meta, rows, rec, yw, xf, xb, zb, v)
    for k in range(3):
        c_far[k] = spread_back(yw, lambda v, j: bx[v, j] if j < 3 else None, -1 - k)


def rest2_body(meta, zn, ze, bx0, bx6, obs, o_low, o_high, zb, xf, xb, yw, c_own, c_part, new):
    for j in range(3, 6):
        for v in range(2):
            rows = [zn[v, j + t] if j + t < 6 else ze[v, j + t - 6] for t in range(7)]
            rec = recorded_row(obs, o_low, o_high, j, v)
            new[v, j - 3] = row_result(meta, rows, rec, yw, xf, xb, zb, v)

    def terms(v, j):
        return bx0[v, j] if j < 3 else new[v, j - 3] if j < 6 else bx6[v, j - 6]

    for row in range(11):
        total = spread_back(yw, terms, row)
        if row < 8:
            c_own[row] = total
        else:
            c_part[row - 8] = total


def final_mid_body(meta, e_a, e_b, c_own, got, out):
    for r in range(3, 8):
        c = c_own[r] if r < 5 else c_own[r] + got[1 - meta[0], 7 - r]
        out[r - 3, :32] = e_a[r - 3] * (0.5 * c[:32])
        out[r - 3, 32:] = e_b[r - 3] * (0.5 * c[32:])


def final_far_body(f_a, f_b, c_own, got, out):
    for r in range(3):
        c = c_own[r] + got[r]
        out[r, :32] = f_a[r + 3] * (0.5 * c[:32])
        out[r, 32:] = f_b[r + 3] * (0.5 * c[32:])


def output_body(meta, far, mid, out):
    def body(core, at):
        for c in range(2):
            block = [far[c, r] if r < 3 else mid[c, r - 3] for r in range(8)]
            block = block if c == 0 else block[::-1]
            out[:, 8 * c : 8 * c + 8, :] = jnp.swapaxes(jnp.stack(block), 0, 1)

    body(0, None)


def on_device(observed, start, spread_z, spread_y, spread_x):
    gy, gz = lax.axis_size("gy"), lax.axis_size("gz")
    across = [(gy + g, g + 1) for g in range(gy - 1)]
    across += [(b, a) for a, b in across]
    up = [(i, i + 1) for i in range(gz - 1)]
    down = [(j, i) for i, j in up]

    def far(x):
        return lax.ppermute(x, ("view", "gy"), across)

    def both(x):
        return lax.all_gather(x, "view")

    def along_z(first, last):
        return lax.ppermute(last, "gz", up), lax.ppermute(first, "gz", down)

    at = lax.axis_index("gz")
    meta = jnp.stack(
        [lax.axis_index("view"), jnp.where(at == 0, 16, 0), jnp.where(at == gz - 1, 80, 96)]
    ).astype(jnp.int32)
    recorded = observed[0]

    (send_far,) = call(far_body, [f32(3, 64, NX)], meta, start)
    f = far(send_far)
    e_a, e_b = call(start_body, [f32(11, 32, NX)] * 2, meta, start)
    e_low, e_high = along_z(e_a, e_b)
    mine, send_a, send_b = call(
        observed_body, [f32(8, 64, NX), f32(4, 64, NX), f32(4, 64, NX)], meta, recorded
    )
    obs, o_first, o_last = call(
        edges_body, [f32(2, 8, 64, NX), f32(2, 8, 16, NX), f32(2, 8, 16, NX)],
        meta, mine, both(send_a), both(send_b),
    )
    o_low, o_high = along_z(o_first, o_last)
    (profiles,) = call(profiles_body, [f32(8, NX)], spread_z, spread_y, spread_x, smem=0)
    zf, zb, xf, xb, yw = call(
        weights_body,
        [b16(384, 256), b16(2, 128, 192), b16(2, 2, 256, 256), b16(2, 2, 256, 256), f32(16, NX)],
        meta, both(profiles),
    )
    obs = (obs, o_low, o_high)
    (ze,) = call(early1_body, [f32(2, 11, 96, NX)], e_a, e_b, e_low, e_high, zf, smem=0)
    f_low, f_high = along_z(*call(faces_body, [f32(3, 32, NX)] * 2, f, ze, smem=0))
    (bx,) = call(middle1_body, [f32(2, 5, 64, NX)], meta, ze, *obs, zb, xf, xb, yw)
    c_far, c_mid, c_part = call(
        late1_body, [f32(6, 64, NX), f32(2, 64, NX), f32(6, 64, NX)],
        meta, f, f_low, f_high, ze, bx, *obs, zf, zb, xf, xb, yw,
        scratch=[pltpu.VMEM((2, 3, 96, NX), F32), pltpu.VMEM((2, 3, 64, NX), F32)],
    )
    got_far = far(c_far)
    got = both(c_part)
    m_a, m_b = call(update_mid_body, [f32(8, 32, NX)] * 2, meta, e_a, e_b, c_mid, c_part, got)
    m_low, m_high = along_z(m_a, m_b)
    ze, bx6 = call(
        early2_body, [f32(2, 6, 96, NX), f32(2, 2, 64, NX)],
        meta, m_a, m_b, m_low, m_high, *obs, zf, zb, xf, xb, yw,
        scratch=[pltpu.VMEM((2, 8, 96, NX), F32)],
    )
    n_a, n_b = call(update_far_body, [f32(6, 32, NX)] * 2, f, e_a, e_b, c_far, got_far, smem=0)
    n_low, n_high = along_z(n_a, n_b)
    c_far, zn, bx0 = call(
        late2_body, [f32(3, 64, NX), f32(2, 6, 96, NX), f32(2, 3, 64, NX)],
        meta, n_a, n_b, n_low, n_high, ze, *obs, zf, zb, xf, xb, yw,
    )
    got_far = far(c_far)
    c_own, c_part = call(
        rest2_body, [f32(8, 64, NX), f32(3, 64, NX)],
        meta, zn, ze, bx0, bx6, *obs, zb, xf, xb, yw,
        scratch=[pltpu.VMEM((2, 3, 64, NX), F32)],
    )
    got_part = both(c_part)
    (mid,) = call(final_mid_body, [f32(5, 64, NX)], meta, m_a, m_b, c_own, got_part)
    other_mid = both(mid)
    (last,) = call(final_far_body, [f32(3, 64, NX)], n_a, n_b, c_own, got_far, smem=0)
    other_last = both(last)
    (out,) = call(output_body, [f32(64, 16, NX)], meta, other_last, other_mid)
    return out


def solution(mesh):
    return jax.shard_map(
        on_device,
        mesh=mesh,
        in_specs=(
            P("view", "gz", "gy", None),
            P("gz", "gy", None),
            P("view", None),
            P("view", None),
            P("view", None),
        ),
        out_specs=P("gz", "gy", None),
        check_vma=False,
    )
```

```python
import jax
import jax.numpy as jnp
from jax import lax
from jax.experimental import pallas as pl
from jax.experimental.pallas import tpu as pltpu
from jax.sharding import PartitionSpec as P

F32 = jnp.float32
BF16 = jnp.bfloat16
NX = 256
LIMIT = 20 * 1024 * 1024
VM = pl.BlockSpec(memory_space=pltpu.VMEM)
SM = pl.BlockSpec(memory_space=pltpu.SMEM)


def call(body, outs, *args, smem=1, flops=0, scratch=()):
    size = sum(a.size * a.dtype.itemsize for a in args)
    size += sum(4 * o.size for o in outs)
    return pl.pallas_call(
        body,
        out_shape=outs,
        in_specs=[SM] * smem + [VM] * (len(args) - smem),
        out_specs=[VM] * len(outs),
        scratch_shapes=list(scratch),
        compiler_params=pltpu.CompilerParams(vmem_limit_bytes=LIMIT),
        cost_estimate=pl.CostEstimate(flops=0, bytes_accessed=0, transcendentals=0),
    )(*args)


def f32(*shape):
    return jax.ShapeDtypeStruct(shape, F32)


def b16(*shape):
    return jax.ShapeDtypeStruct(shape, BF16)


def parts(x):
    high = x.astype(BF16)
    return high, (x - high.astype(F32)).astype(BF16)


def dot(a, b):
    return jnp.dot(a, b, preferred_element_type=F32)


def rows_of(ref, half):
    return jnp.swapaxes(ref[:, 8 * half : 8 * half + 8, :], 0, 1)


def by_core(meta, body):
    for core in range(2):
        pl.when(meta[0] == core)(lambda core=core: body(core, lambda r: r % 8 if core == 0 else 7 - r % 8))


def far_body(meta, start, out):
    def body(core, at):
        rows = rows_of(start, core)
        for j in range(3):
            out[j] = rows[at(j)]

    by_core(meta, body)


def start_body(meta, start, e_a, e_b):
    def body(core, at):
        rows = (rows_of(start, core), rows_of(start, 1 - core))
        for j in range(11):
            e_a[j] = rows[j // 8][at(j), :32]
            e_b[j] = rows[j // 8][at(j), 32:]

    by_core(meta, body)


def observed_body(meta, observed, mine, send_a, send_b):
    def body(core, at):
        rows, others = rows_of(observed, core), rows_of(observed, 1 - core)
        for j in range(8):
            mine[j] = rows[at(j)]
            if j < 4:
                send_a[j] = others[at(15 - j)]
            else:
                send_b[j - 4] = others[at(15 - j)]

    by_core(meta, body)


def profiles_body(sz, sy, sx, out):
    out[...] = jnp.zeros((8, NX), F32)
    out[0:1, 0:31] = sz[...]
    out[1:2, 0:7] = sy[...]
    out[2:3, 0:7] = sx[...]


def edges_body(meta, mine, got_a, got_b, obs, low, high):
    other = 1 - meta[0]
    for j in range(8):
        for v, row in ((meta[0], mine[j]), (other, got_a[other, j] if j < 4 else got_b[other, j - 4])):
            obs[v, j] = row
            low[v, j] = row[0:16]
            high[v, j] = row[48:64]


def faces_body(far, _, first, last):
    for j in range(3):
        first[j] = far[j, 0:32]
        last[j] = far[j, 32:64]


def weights_body(meta, both, zf, zb, xf, xb, yw):
    def band(shape, row, taps, place):
        d = lax.broadcasted_iota(jnp.int32, shape, 1) - lax.broadcasted_iota(jnp.int32, shape, 0)
        total = jnp.zeros(shape, F32)
        for t in range(taps):
            total = jnp.where(d == place(t), row[:, t : t + 1], total)
        return total

    for v in range(2):
        w = both[v]
        sums = jnp.sum(w, axis=1, keepdims=True)
        w = w / sums_or_one(sums)
        wz, wy, wx = w[0:1], w[1:2], w[2:3]
        high, low = parts(band((96, 128), wz, 31, lambda t: t + 1))
        zf[192 * v : 192 * v + 96, 0:128] = high
        zf[192 * v : 192 * v + 96, 128:256] = high
        zf[192 * v + 96 : 192 * v + 192, 0:128] = low
        zf[192 * v + 96 : 192 * v + 192, 128:256] = jnp.zeros((96, 128), BF16)
        high, low = parts(band((64, 96), wz, 31, lambda t: 31 - t))
        zb[v, 0:64] = jnp.concatenate([high, high], axis=1)
        zb[v, 64:128] = jnp.concatenate([low, jnp.zeros((64, 96), BF16)], axis=1)
        high, low = parts(band((256, 256), wx, 7, lambda t: 3 - t))
        xf[v, 0] = high
        xf[v, 1] = low
        high, low = parts(band((256, 256), wx, 7, lambda t: t - 3))
        xb[v, 0] = high
        xb[v, 1] = low
        for core in range(2):

            @pl.when(meta[0] == core)
            def _(core=core, v=v, wy=wy):
                for t in range(7):
                    s = t if core == 0 else 6 - t
                    yw[8 * v + t : 8 * v + t + 1, :] = jnp.broadcast_to(wy[:, s : s + 1], (1, NX))

        yw[8 * v + 7 : 8 * v + 8, :] = jnp.zeros((1, NX), F32)


def sums_or_one(sums):
    rows = lax.broadcasted_iota(jnp.int32, sums.shape, 0)
    return jnp.where(rows < 3, sums, 1.0)


def blur_z(zf, low, a, b, high):
    highs, lows = zip(*[parts(x) for x in (low, a, b, high)])
    both = dot(zf[...], jnp.concatenate(highs + lows, axis=0))
    return [both[192 * v : 192 * v + 96] + both[192 * v + 96 : 192 * v + 192] for v in range(2)]


def blur_x(x, weight, v):
    high, low = parts(x)
    return dot(high, weight[v, 0]) + dot(low, weight[v, 0]) + dot(high, weight[v, 1])


def row_results(meta, rows, recorded, yw, xf, xb, zb, v):
    totals = []
    for about in rows:
        total = yw[8 * v : 8 * v + 1] * about[0]
        for t in range(1, 7):
            total = total + yw[8 * v + t : 8 * v + t + 1] * about[t]
        totals.append(total)
    blurred = blur_x(jnp.concatenate(totals, axis=0), xf, v)
    at = lax.broadcasted_iota(jnp.int32, (96, NX), 0)
    inside = (at >= meta[1]) & (at < meta[2])
    back = []
    for k, rec in enumerate(recorded):
        quotient = rec / jnp.where(inside, blurred[96 * k : 96 * k + 96], 1.0)
        both = dot(zb[v], jnp.concatenate(parts(quotient), axis=0))
        back.append(both[0:64] + both[64:128])
    back = blur_x(jnp.concatenate(back, axis=0), xb, v)
    return [back[64 * k : 64 * k + 64] for k in range(len(rows))]


def recorded_row(obs, o_low, o_high, j, v):
    return jnp.concatenate([o_low[v, j], obs[v, j], o_high[v, j]], axis=0)


def spread_back(yw, terms, row, planes=slice(0, 64)):
    total = None
    for v in range(2):
        for t in range(7):
            j = row + t - 3
            if 0 <= j <= 7:
                term = yw[8 * v + 6 - t : 8 * v + 7 - t] * terms(v, j)[planes]
                total = term if total is None else total + term
    return total


def early1_body(e_a, e_b, e_low, e_high, zf, ze):
    for r in range(11):
        for v, x in enumerate(blur_z(zf, e_low[r], e_a[r], e_b[r], e_high[r])):
            ze[v, r] = x


def middle1_body(meta, ze, obs, o_low, o_high, zb, xf, xb, yw, bx):
    for v in range(2):
        rows = [[ze[v, k + t] for t in range(7)] for k in range(5)]
        recs = [recorded_row(obs, o_low, o_high, j, v) for j in range(3, 8)]
        for k, x in enumerate(row_results(meta, rows, recs, yw, xf, xb, zb, v)):
            bx[v, k] = x


def late1_body(meta, f, f_low, f_high, ze, bx, obs, o_low, o_high, zf, zb, xf, xb, yw,
               c_far, c_mid, c_part, buf, new):
    for j in range(3):
        for v, x in enumerate(blur_z(zf, f_low[j], f[j, :32], f[j, 32:], f_high[j])):
            buf[v, 2 - j] = x
    for v in range(2):
        rows = [[buf[v, j + t] if j + t < 3 else ze[v, j + t - 3] for t in range(7)] for j in range(3)]
        recs = [recorded_row(obs, o_low, o_high, j, v) for j in range(3)]
        for j, x in enumerate(row_results(meta, rows, recs, yw, xf, xb, zb, v)):
            new[v, j] = x

    def terms(v, j):
        return new[v, j] if j < 3 else bx[v, j - 3]

    for row in range(-3, 11):
        total = spread_back(yw, terms, row)
        if row < 3:
            c_far[row + 3] = total
        elif row < 5:
            c_mid[row - 3] = total
        else:
            c_part[row - 5] = total


def update_mid_body(meta, e_a, e_b, c_mid, c_part, got, out_a, out_b):
    for r in range(3, 11):
        c = c_mid[r - 3] if r < 5 else c_part[r - 5] + got[1 - meta[0], 10 - r]
        out_a[r - 3] = e_a[r] * (0.5 * c[:32])
        out_b[r - 3] = e_b[r] * (0.5 * c[32:])


def update_far_body(far, e_a, e_b, c, got, out_a, out_b):
    for r in range(-3, 3):
        factor = 0.5 * (c[r + 3] + got[2 - r])
        out_a[r + 3] = (far[-1 - r, :32] if r < 0 else e_a[r]) * factor[:32]
        out_b[r + 3] = (far[-1 - r, 32:] if r < 0 else e_b[r]) * factor[32:]


def early2_body(meta, e_a, e_b, e_low, e_high, obs, o_low, o_high, zf, zb, xf, xb, yw, ze, bx, buf):
    for r in range(8):
        for v, x in enumerate(blur_z(zf, e_low[r], e_a[r], e_b[r], e_high[r])):
            buf[v, r] = x
            if r < 6:
                ze[v, r] = x
    for v in range(2):
        rows = [[buf[v, k + t] for t in range(7)] for k in range(2)]
        recs = [recorded_row(obs, o_low, o_high, j, v) for j in (6, 7)]
        for k, x in enumerate(row_results(meta, rows, recs, yw, xf, xb, zb, v)):
            bx[v, k] = x


def late2_body(meta, f_a, f_b, f_low, f_high, ze, obs, o_low, o_high, zf, zb, xf, xb, yw,
               c_far, zn, bx):
    for r in range(6):
        for v, x in enumerate(blur_z(zf, f_low[r], f_a[r], f_b[r], f_high[r])):
            zn[v, r] = x
    for v in range(2):
        rows = [[zn[v, j + t] if j + t < 6 else ze[v, j + t - 6] for t in range(7)] for j in range(3)]
        recs = [recorded_row(obs, o_low, o_high, j, v) for j in range(3)]
        for j, x in enumerate(row_results(meta, rows, recs, yw, xf, xb, zb, v)):
            bx[v, j] = x
    for k in range(3):
        c_far[k] = spread_back(yw, lambda v, j: bx[v, j] if j < 3 else None, -1 - k)


def rest2_body(meta, zn, ze, bx0, bx6, obs, o_low, o_high, zb, xf, xb, yw, c_own, c_part, new):
    for v in range(2):
        rows = [[zn[v, j + t] if j + t < 6 else ze[v, j + t - 6] for t in range(7)] for j in range(3, 6)]
        recs = [recorded_row(obs, o_low, o_high, j, v) for j in range(3, 6)]
        for k, x in enumerate(row_results(meta, rows, recs, yw, xf, xb, zb, v)):
            new[v, k] = x

    def terms(v, j):
        return bx0[v, j] if j < 3 else new[v, j - 3] if j < 6 else bx6[v, j - 6]

    for row in range(11):
        total = spread_back(yw, terms, row)
        if row < 8:
            c_own[row] = total
        else:
            c_part[row - 8] = total


def final_mid_body(meta, e_a, e_b, c_own, got, out):
    for r in range(3, 8):
        c = c_own[r] if r < 5 else c_own[r] + got[1 - meta[0], 7 - r]
        out[r - 3, :32] = e_a[r - 3] * (0.5 * c[:32])
        out[r - 3, 32:] = e_b[r - 3] * (0.5 * c[32:])


def final_far_body(f_a, f_b, c_own, got, out):
    for r in range(3):
        c = c_own[r] + got[r]
        out[r, :32] = f_a[r + 3] * (0.5 * c[:32])
        out[r, 32:] = f_b[r + 3] * (0.5 * c[32:])


def output_body(meta, far, mid, out):
    def body(core, at):
        for c in range(2):
            block = [far[c, r] if r < 3 else mid[c, r - 3] for r in range(8)]
            block = block if c == 0 else block[::-1]
            out[:, 8 * c : 8 * c + 8, :] = jnp.swapaxes(jnp.stack(block), 0, 1)

    body(0, None)


def on_device(observed, start, spread_z, spread_y, spread_x):
    gy, gz = lax.axis_size("gy"), lax.axis_size("gz")
    across = [(gy + g, g + 1) for g in range(gy - 1)]
    across += [(b, a) for a, b in across]
    up = [(i, i + 1) for i in range(gz - 1)]
    down = [(j, i) for i, j in up]

    def far(x):
        return lax.ppermute(x, ("view", "gy"), across)

    def both(x):
        return lax.all_gather(x, "view")

    def along_z(first, last):
        return lax.ppermute(last, "gz", up), lax.ppermute(first, "gz", down)

    at = lax.axis_index("gz")
    meta = jnp.stack(
        [lax.axis_index("view"), jnp.where(at == 0, 16, 0), jnp.where(at == gz - 1, 80, 96)]
    ).astype(jnp.int32)
    recorded = observed[0]

    (send_far,) = call(far_body, [f32(3, 64, NX)], meta, start)
    f = far(send_far)
    e_a, e_b = call(start_body, [f32(11, 32, NX)] * 2, meta, start)
    e_low, e_high = along_z(e_a, e_b)
    mine, send_a, send_b = call(
        observed_body, [f32(8, 64, NX), f32(4, 64, NX), f32(4, 64, NX)], meta, recorded
    )
    obs, o_first, o_last = call(
        edges_body, [f32(2, 8, 64, NX), f32(2, 8, 16, NX), f32(2, 8, 16, NX)],
        meta, mine, both(send_a), both(send_b),
    )
    o_low, o_high = along_z(o_first, o_last)
    (profiles,) = call(profiles_body, [f32(8, NX)], spread_z, spread_y, spread_x, smem=0)
    zf, zb, xf, xb, yw = call(
        weights_body,
        [b16(384, 256), b16(2, 128, 192), b16(2, 2, 256, 256), b16(2, 2, 256, 256), f32(16, NX)],
        meta, both(profiles),
    )
    obs = (obs, o_low, o_high)
    (ze,) = call(early1_body, [f32(2, 11, 96, NX)], e_a, e_b, e_low, e_high, zf, smem=0)
    f_low, f_high = along_z(*call(faces_body, [f32(3, 32, NX)] * 2, f, ze, smem=0))
    (bx,) = call(middle1_body, [f32(2, 5, 64, NX)], meta, ze, *obs, zb, xf, xb, yw)
    c_far, c_mid, c_part = call(
        late1_body, [f32(6, 64, NX), f32(2, 64, NX), f32(6, 64, NX)],
        meta, f, f_low, f_high, ze, bx, *obs, zf, zb, xf, xb, yw,
        scratch=[pltpu.VMEM((2, 3, 96, NX), F32), pltpu.VMEM((2, 3, 64, NX), F32)],
    )
    got_far = far(c_far)
    got = both(c_part)
    m_a, m_b = call(update_mid_body, [f32(8, 32, NX)] * 2, meta, e_a, e_b, c_mid, c_part, got)
    m_low, m_high = along_z(m_a, m_b)
    ze, bx6 = call(
        early2_body, [f32(2, 6, 96, NX), f32(2, 2, 64, NX)],
        meta, m_a, m_b, m_low, m_high, *obs, zf, zb, xf, xb, yw,
        scratch=[pltpu.VMEM((2, 8, 96, NX), F32)],
    )
    n_a, n_b = call(update_far_body, [f32(6, 32, NX)] * 2, f, e_a, e_b, c_far, got_far, smem=0)
    n_low, n_high = along_z(n_a, n_b)
    c_far, zn, bx0 = call(
        late2_body, [f32(3, 64, NX), f32(2, 6, 96, NX), f32(2, 3, 64, NX)],
        meta, n_a, n_b, n_low, n_high, ze, *obs, zf, zb, xf, xb, yw,
    )
    got_far = far(c_far)
    c_own, c_part = call(
        rest2_body, [f32(8, 64, NX), f32(3, 64, NX)],
        meta, zn, ze, bx0, bx6, *obs, zb, xf, xb, yw,
        scratch=[pltpu.VMEM((2, 3, 64, NX), F32)],
    )
    got_part = both(c_part)
    (mid,) = call(final_mid_body, [f32(5, 64, NX)], meta, m_a, m_b, c_own, got_part)
    other_mid = both(mid)
    (last,) = call(final_far_body, [f32(3, 64, NX)], n_a, n_b, c_own, got_far, smem=0)
    other_last = both(last)
    (out,) = call(output_body, [f32(64, 16, NX)], meta, other_last, other_mid)
    return out


def solution(mesh):
    return jax.shard_map(
        on_device,
        mesh=mesh,
        in_specs=(
            P("view", "gz", "gy", None),
            P("gz", "gy", None),
            P("view", None),
            P("view", None),
            P("view", None),
        ),
        out_specs=P("gz", "gy", None),
        check_vma=False,
    )
```

```python
import jax
import jax.numpy as jnp
from jax import lax
from jax.experimental import pallas as pl
from jax.experimental.pallas import tpu as pltpu
from jax.sharding import PartitionSpec as P

F32 = jnp.float32
BF16 = jnp.bfloat16
NX = 256
LIMIT = 20 * 1024 * 1024
VM = pl.BlockSpec(memory_space=pltpu.VMEM)
SM = pl.BlockSpec(memory_space=pltpu.SMEM)


def call(body, outs, *args, smem=1, flops=0, scratch=()):
    size = sum(a.size * a.dtype.itemsize for a in args)
    size += sum(4 * o.size for o in outs)
    return pl.pallas_call(
        body,
        out_shape=outs,
        in_specs=[SM] * smem + [VM] * (len(args) - smem),
        out_specs=[VM] * len(outs),
        scratch_shapes=list(scratch),
        compiler_params=pltpu.CompilerParams(vmem_limit_bytes=LIMIT),
        cost_estimate=pl.CostEstimate(flops=0, bytes_accessed=0, transcendentals=0),
    )(*args)


def f32(*shape):
    return jax.ShapeDtypeStruct(shape, F32)


def b16(*shape):
    return jax.ShapeDtypeStruct(shape, BF16)


def parts(x):
    high = x.astype(BF16)
    return high, (x - high.astype(F32)).astype(BF16)


def dot(a, b):
    return jnp.dot(a, b, preferred_element_type=F32)


def rows_of(ref, half):
    return jnp.swapaxes(ref[:, 8 * half : 8 * half + 8, :], 0, 1)


def by_core(meta, body):
    for core in range(2):
        pl.when(meta[0] == core)(lambda core=core: body(core, lambda r: r % 8 if core == 0 else 7 - r % 8))


def far_body(meta, start, out, half, sem):
    def body(core, at):
        copy = pltpu.make_async_copy(start.at[:, 8 * core : 8 * core + 8, :], half, sem)
        copy.start()
        copy.wait()
        rows = jnp.swapaxes(half[...], 0, 1)
        for j in range(3):
            out[j] = rows[at(j)]

    by_core(meta, body)


def start_body(meta, start, e_a, e_b):
    def body(core, at):
        rows = (rows_of(start, core), rows_of(start, 1 - core))
        for j in range(11):
            e_a[j] = rows[j // 8][at(j), :32]
            e_b[j] = rows[j // 8][at(j), 32:]

    by_core(meta, body)


def observed_body(meta, observed, mine, send_a, send_b):
    def body(core, at):
        rows, others = rows_of(observed, core), rows_of(observed, 1 - core)
        for j in range(8):
            mine[j] = rows[at(j)]
            if j < 4:
                send_a[j] = others[at(15 - j)]
            else:
                send_b[j - 4] = others[at(15 - j)]

    by_core(meta, body)


def profiles_body(sz, sy, sx, out):
    out[...] = jnp.zeros((8, NX), F32)
    out[0:1, 0:31] = sz[...]
    out[1:2, 0:7] = sy[...]
    out[2:3, 0:7] = sx[...]


def edges_body(meta, mine, got_a, got_b, obs, low, high):
    other = 1 - meta[0]
    for j in range(8):
        for v, row in ((meta[0], mine[j]), (other, got_a[other, j] if j < 4 else got_b[other, j - 4])):
            obs[v, j] = row
            low[v, j] = row[0:16]
            high[v, j] = row[48:64]


def faces_body(far, _, first, last):
    for j in range(3):
        first[j] = far[j, 0:32]
        last[j] = far[j, 32:64]


def weights_body(meta, both, zf, zb, xf, xb, yw):
    def band(shape, row, taps, place):
        d = lax.broadcasted_iota(jnp.int32, shape, 1) - lax.broadcasted_iota(jnp.int32, shape, 0)
        total = jnp.zeros(shape, F32)
        for t in range(taps):
            total = jnp.where(d == place(t), row[:, t : t + 1], total)
        return total

    for v in range(2):
        w = both[v]
        sums = jnp.sum(w, axis=1, keepdims=True)
        w = w / sums_or_one(sums)
        wz, wy, wx = w[0:1], w[1:2], w[2:3]
        high, low = parts(band((96, 128), wz, 31, lambda t: t + 1))
        zf[192 * v : 192 * v + 96, 0:128] = high
        zf[192 * v : 192 * v + 96, 128:256] = high
        zf[192 * v + 96 : 192 * v + 192, 0:128] = low
        zf[192 * v + 96 : 192 * v + 192, 128:256] = jnp.zeros((96, 128), BF16)
        high, low = parts(band((64, 96), wz, 31, lambda t: 31 - t))
        zb[v, 0:64] = jnp.concatenate([high, high], axis=1)
        zb[v, 64:128] = jnp.concatenate([low, jnp.zeros((64, 96), BF16)], axis=1)
        high, low = parts(band((256, 256), wx, 7, lambda t: 3 - t))
        xf[v, 0] = high
        xf[v, 1] = low
        high, low = parts(band((256, 256), wx, 7, lambda t: t - 3))
        xb[v, 0] = high
        xb[v, 1] = low
        for core in range(2):

            @pl.when(meta[0] == core)
            def _(core=core, v=v, wy=wy):
                for t in range(7):
                    s = t if core == 0 else 6 - t
                    yw[8 * v + t : 8 * v + t + 1, :] = jnp.broadcast_to(wy[:, s : s + 1], (1, NX))

        yw[8 * v + 7 : 8 * v + 8, :] = jnp.zeros((1, NX), F32)


def sums_or_one(sums):
    rows = lax.broadcasted_iota(jnp.int32, sums.shape, 0)
    return jnp.where(rows < 3, sums, 1.0)


def blur_z(zf, low, a, b, high):
    highs, lows = zip(*[parts(x) for x in (low, a, b, high)])
    both = dot(zf[...], jnp.concatenate(highs + lows, axis=0))
    return [both[192 * v : 192 * v + 96] + both[192 * v + 96 : 192 * v + 192] for v in range(2)]


def blur_x(x, weight, v):
    high, low = parts(x)
    return dot(high, weight[v, 0]) + dot(low, weight[v, 0]) + dot(high, weight[v, 1])


def row_results(meta, rows, recorded, yw, xf, xb, zb, v):
    totals = []
    for about in rows:
        total = yw[8 * v : 8 * v + 1] * about[0]
        for t in range(1, 7):
            total = total + yw[8 * v + t : 8 * v + t + 1] * about[t]
        totals.append(total)
    blurred = blur_x(jnp.concatenate(totals, axis=0), xf, v)
    at = lax.broadcasted_iota(jnp.int32, (96, NX), 0)
    inside = (at >= meta[1]) & (at < meta[2])
    back = []
    for k, rec in enumerate(recorded):
        quotient = rec / jnp.where(inside, blurred[96 * k : 96 * k + 96], 1.0)
        both = dot(zb[v], jnp.concatenate(parts(quotient), axis=0))
        back.append(both[0:64] + both[64:128])
    back = blur_x(jnp.concatenate(back, axis=0), xb, v)
    return [back[64 * k : 64 * k + 64] for k in range(len(rows))]


def recorded_row(obs, o_low, o_high, j, v):
    return jnp.concatenate([o_low[v, j], obs[v, j], o_high[v, j]], axis=0)


def spread_back(yw, terms, row, planes=slice(0, 64)):
    total = None
    for v in range(2):
        for t in range(7):
            j = row + t - 3
            if 0 <= j <= 7:
                term = yw[8 * v + 6 - t : 8 * v + 7 - t] * terms(v, j)[planes]
                total = term if total is None else total + term
    return total


def early1_body(e_a, e_b, e_low, e_high, zf, ze):
    for r in range(11):
        for v, x in enumerate(blur_z(zf, e_low[r], e_a[r], e_b[r], e_high[r])):
            ze[v, r] = x


def middle1_body(meta, ze, obs, o_low, o_high, zb, xf, xb, yw, bx):
    for v in range(2):
        rows = [[ze[v, k + t] for t in range(7)] for k in range(3)]
        recs = [recorded_row(obs, o_low, o_high, j, v) for j in range(3, 6)]
        for k, x in enumerate(row_results(meta, rows, recs, yw, xf, xb, zb, v)):
            bx[v, k] = x


def late1_body(meta, f, f_low, f_high, ze, bx, obs, o_low, o_high, zf, zb, xf, xb, yw,
               c_far, new, buf):
    for j in range(3):
        for v, x in enumerate(blur_z(zf, f_low[j], f[j, :32], f[j, 32:], f_high[j])):
            buf[v, 2 - j] = x
    for v in range(2):
        rows = [[buf[v, j + t] if j + t < 3 else ze[v, j + t - 3] for t in range(7)] for j in range(3)]
        recs = [recorded_row(obs, o_low, o_high, j, v) for j in range(3)]
        for j, x in enumerate(row_results(meta, rows, recs, yw, xf, xb, zb, v)):
            new[v, j] = x

    for row in range(-3, 3):
        c_far[row + 3] = spread_back(yw, lambda v, j: new[v, j] if j < 3 else bx[v, j - 3], row)


def rest1_body(meta, ze, bx0, bx3, obs, o_low, o_high, zb, xf, xb, yw, c_mid, c_part, new):
    for v in range(2):
        rows = [[ze[v, k + t] for t in range(7)] for k in (3, 4)]
        recs = [recorded_row(obs, o_low, o_high, j, v) for j in (6, 7)]
        for k, x in enumerate(row_results(meta, rows, recs, yw, xf, xb, zb, v)):
            new[v, k] = x

    def terms(v, j):
        return bx0[v, j] if j < 3 else bx3[v, j - 3] if j < 6 else new[v, j - 6]

    for row in range(3, 11):
        total = spread_back(yw, terms, row)
        if row < 5:
            c_mid[row - 3] = total
        else:
            c_part[row - 5] = total


def update_mid_body(meta, e_a, e_b, c_mid, c_part, got, out_a, out_b, first, last):
    for r in range(3, 11):
        c = c_mid[r - 3] if r < 5 else c_part[r - 5] + got[1 - meta[0], 10 - r]
        new_a, new_b = e_a[r] * (0.5 * c[:32]), e_b[r] * (0.5 * c[32:])
        out_a[r - 3] = new_a
        out_b[r - 3] = new_b
        if r < 8:
            first[r - 3] = new_a
            last[r - 3] = new_b


def halo_body(low, high, out):
    for j in range(3):
        out[j, 0:32] = low[j + 2]
        out[j, 32:64] = high[j + 2]


def update_far_body(far, e_a, e_b, c, got, out_a, out_b):
    for r in range(-3, 3):
        factor = 0.5 * (c[r + 3] + got[2 - r])
        out_a[r + 3] = (far[-1 - r, :32] if r < 0 else e_a[r]) * factor[:32]
        out_b[r + 3] = (far[-1 - r, 32:] if r < 0 else e_b[r]) * factor[32:]


def early2_body(meta, e_a, e_b, e_low, e_high, got, obs, o_low, o_high, zf, zb, xf, xb, yw, ze, bx, buf):
    for r in range(8):
        if r < 5:
            low, high = e_low[r], e_high[r]
        else:
            low, high = got[1 - meta[0], 7 - r, 0:32], got[1 - meta[0], 7 - r, 32:64]
        for v, x in enumerate(blur_z(zf, low, e_a[r], e_b[r], high)):
            buf[v, r] = x
            if r < 6:
                ze[v, r] = x
    for v in range(2):
        rows = [[buf[v, k + t] for t in range(7)] for k in range(2)]
        recs = [recorded_row(obs, o_low, o_high, j, v) for j in (6, 7)]
        for k, x in enumerate(row_results(meta, rows, recs, yw, xf, xb, zb, v)):
            bx[v, k] = x


def late2_body(meta, f_a, f_b, f_low, f_high, ze, obs, o_low, o_high, zf, zb, xf, xb, yw,
               c_far, zn, bx):
    for r in range(6):
        for v, x in enumerate(blur_z(zf, f_low[r], f_a[r], f_b[r], f_high[r])):
            zn[v, r] = x
    for v in range(2):
        rows = [[zn[v, j + t] if j + t < 6 else ze[v, j + t - 6] for t in range(7)] for j in range(3)]
        recs = [recorded_row(obs, o_low, o_high, j, v) for j in range(3)]
        for j, x in enumerate(row_results(meta, rows, recs, yw, xf, xb, zb, v)):
            bx[v, j] = x
    for k in range(3):
        c_far[k] = spread_back(yw, lambda v, j: bx[v, j] if j < 3 else None, -1 - k)


def rest2_body(meta, zn, ze, bx0, bx6, obs, o_low, o_high, zb, xf, xb, yw, c_own, c_part, new):
    for v in range(2):
        rows = [[zn[v, j + t] if j + t < 6 else ze[v, j + t - 6] for t in range(7)] for j in range(3, 6)]
        recs = [recorded_row(obs, o_low, o_high, j, v) for j in range(3, 6)]
        for k, x in enumerate(row_results(meta, rows, recs, yw, xf, xb, zb, v)):
            new[v, k] = x

    def terms(v, j):
        return bx0[v, j] if j < 3 else new[v, j - 3] if j < 6 else bx6[v, j - 6]

    for row in range(11):
        total = spread_back(yw, terms, row)
        if row < 8:
            c_own[row] = total
        else:
            c_part[row - 8] = total


def final_mid_body(meta, e_a, e_b, c_own, got, out):
    for r in range(3, 8):
        c = c_own[r] if r < 5 else c_own[r] + got[1 - meta[0], 7 - r]
        out[r - 3, :32] = e_a[r - 3] * (0.5 * c[:32])
        out[r - 3, 32:] = e_b[r - 3] * (0.5 * c[32:])


def final_far_body(f_a, f_b, c_own, got, out):
    for r in range(3):
        c = c_own[r] + got[r]
        out[r, :32] = f_a[r + 3] * (0.5 * c[:32])
        out[r, 32:] = f_b[r + 3] * (0.5 * c[32:])


def output_body(far, mid, out):
    planes = pl.ds(pl.multiple_of(16 * pl.program_id(0), 16), 16)
    for c in range(2):
        block = [far[c, r, planes] if r < 3 else mid[c, r - 3, planes] for r in range(8)]
        block = block if c == 0 else block[::-1]
        out[:, 8 * c : 8 * c + 8, :] = jnp.swapaxes(jnp.stack(block), 0, 1)


def on_device(observed, start, spread_z, spread_y, spread_x):
    gy, gz = lax.axis_size("gy"), lax.axis_size("gz")
    across = [(gy + g, g + 1) for g in range(gy - 1)]
    across += [(b, a) for a, b in across]
    up = [(i, i + 1) for i in range(gz - 1)]
    down = [(j, i) for i, j in up]

    def far(x):
        return lax.ppermute(x, ("view", "gy"), across)

    def both(x):
        return lax.all_gather(x, "view")

    def along_z(first, last):
        return lax.ppermute(last, "gz", up), lax.ppermute(first, "gz", down)

    at = lax.axis_index("gz")
    meta = jnp.stack(
        [lax.axis_index("view"), jnp.where(at == 0, 16, 0), jnp.where(at == gz - 1, 80, 96)]
    ).astype(jnp.int32)
    recorded = observed[0]

    send_far = pl.pallas_call(
        far_body,
        out_shape=f32(3, 64, NX),
        in_specs=[SM, pl.BlockSpec(memory_space=pltpu.HBM)],
        out_specs=VM,
        scratch_shapes=[pltpu.VMEM((64, 8, NX), F32), pltpu.SemaphoreType.DMA(())],
        compiler_params=pltpu.CompilerParams(vmem_limit_bytes=60 * 1024 * 1024),
    )(meta, start)
    f = far(send_far)
    e_a, e_b = call(start_body, [f32(11, 32, NX)] * 2, meta, start)
    e_low, e_high = along_z(e_a, e_b)
    mine, send_a, send_b = call(
        observed_body, [f32(8, 64, NX), f32(4, 64, NX), f32(4, 64, NX)], meta, recorded
    )
    obs, o_first, o_last = call(
        edges_body, [f32(2, 8, 64, NX), f32(2, 8, 16, NX), f32(2, 8, 16, NX)],
        meta, mine, both(send_a), both(send_b),
    )
    o_low, o_high = along_z(o_first, o_last)
    (profiles,) = call(profiles_body, [f32(8, NX)], spread_z, spread_y, spread_x, smem=0)
    zf, zb, xf, xb, yw = call(
        weights_body,
        [b16(384, 256), b16(2, 128, 192), b16(2, 2, 256, 256), b16(2, 2, 256, 256), f32(16, NX)],
        meta, both(profiles),
    )
    obs = (obs, o_low, o_high)
    (ze,) = call(early1_body, [f32(2, 11, 96, NX)], e_a, e_b, e_low, e_high, zf, smem=0)
    f_low, f_high = along_z(*call(faces_body, [f32(3, 32, NX)] * 2, f, ze, smem=0))
    (bx,) = call(middle1_body, [f32(2, 3, 64, NX)], meta, ze, *obs, zb, xf, xb, yw)
    c_far, bx0 = call(
        late1_body, [f32(6, 64, NX), f32(2, 3, 64, NX)],
        meta, f, f_low, f_high, ze, bx, *obs, zf, zb, xf, xb, yw,
        scratch=[pltpu.VMEM((2, 3, 96, NX), F32)],
    )
    got_far = far(c_far)
    c_mid, c_part = call(
        rest1_body, [f32(2, 64, NX), f32(6, 64, NX)],
        meta, ze, bx0, bx, *obs, zb, xf, xb, yw,
        scratch=[pltpu.VMEM((2, 2, 64, NX), F32)],
    )
    got = both(c_part)
    m_a, m_b, first, last = call(
        update_mid_body, [f32(8, 32, NX)] * 2 + [f32(5, 32, NX)] * 2, meta, e_a, e_b, c_mid, c_part, got)
    m_low, m_high = along_z(first, last)
    (halo,) = call(halo_body, [f32(3, 64, NX)], m_low, m_high, smem=0)
    ze, bx6 = call(
        early2_body, [f32(2, 6, 96, NX), f32(2, 2, 64, NX)],
        meta, m_a, m_b, m_low, m_high, both(halo), *obs, zf, zb, xf, xb, yw,
        scratch=[pltpu.VMEM((2, 8, 96, NX), F32)],
    )
    n_a, n_b = call(update_far_body, [f32(6, 32, NX)] * 2, f, e_a, e_b, c_far, got_far, smem=0)
    n_low, n_high = along_z(n_a, n_b)
    c_far, zn, bx0 = call(
        late2_body, [f32(3, 64, NX), f32(2, 6, 96, NX), f32(2, 3, 64, NX)],
        meta, n_a, n_b, n_low, n_high, ze, *obs, zf, zb, xf, xb, yw,
    )
    got_far = far(c_far)
    c_own, c_part = call(
        rest2_body, [f32(8, 64, NX), f32(3, 64, NX)],
        meta, zn, ze, bx0, bx6, *obs, zb, xf, xb, yw,
        scratch=[pltpu.VMEM((2, 3, 64, NX), F32)],
    )
    got_part = both(c_part)
    (mid,) = call(final_mid_body, [f32(5, 64, NX)], meta, m_a, m_b, c_own, got_part)
    other_mid = both(mid)
    (last,) = call(final_far_body, [f32(3, 64, NX)], n_a, n_b, c_own, got_far, smem=0)
    other_last = both(last)
    return pl.pallas_call(
        output_body,
        out_shape=f32(64, 16, NX),
        grid=(4,),
        in_specs=[VM, VM],
        out_specs=pl.BlockSpec((16, 16, NX), lambda i: (i, 0, 0)),
        compiler_params=pltpu.CompilerParams(vmem_limit_bytes=LIMIT),
    )(other_last, other_mid)


def solution(mesh):
    return jax.shard_map(
        on_device,
        mesh=mesh,
        in_specs=(
            P("view", "gz", "gy", None),
            P("gz", "gy", None),
            P("view", None),
            P("view", None),
            P("view", None),
        ),
        out_specs=P("gz", "gy", None),
        check_vma=False,
    )
```
